512 devices in a mesh: ctx: 64 (over x, z, core), head: 8 (over y).
Axes of the slice: x: 4, y: 8, z: 8, core: 2. Of those that a mesh axis runs over, the one named last changes fastest.
Arguments:
- queries: bfloat16 [16384, 64, 128], P('ctx', 'head'), may hold values from -5 to 5
- keys: bfloat16 [16384, 64, 128], P('ctx', 'head'), may hold values from -5 to 5
- values: bfloat16 [16384, 64, 128], P('ctx', 'head'), may hold values from -6 to 6
- selected: int32 [64, 3], P('ctx'), may hold values from 0 to 62, as said below
Outputs:
- attended: bfloat16 [16384, 8192], P(('ctx', 'head'))
The draws below stay inside these ranges and needn't reach their ends.
Inputs may be any that keep to these rules, and one draw needn't show every extreme that they name: Row q of selected names 3 key blocks for query block q. For q >= 1 it names block q - 1, and its other entries are distinct blocks below q; where fewer than 3 blocks lie below q, the remaining entries equal q and add nothing. Some blocks are named by far more rows than others.
All inputs are finite; a program needn't handle non-finite values.
Results may differ from the reference program's by a relative error of at most 0.0045.
Values may be sent and summed in bfloat16 or wider, within the bound.
A program may use at most 64 MiB of HBM per device.

```python
import jax
import jax.numpy as jnp
from jax import lax

HEAD_DIM = 128
BLOCK = 256
TOPK = 3
HEADS = 64
TOKENS = 16384
NB = 64


def draw_queries(key, part):
    key = jax.random.fold_in(key, 1)
    return jnp.clip(jax.random.normal(key, (TOKENS, HEADS, HEAD_DIM), jnp.float32), -5.0, 5.0).astype(jnp.bfloat16)


def draw_keys(key, part):
    key = jax.random.fold_in(key, 2)
    return jnp.clip(jax.random.normal(key, (TOKENS, HEADS, HEAD_DIM), jnp.float32), -5.0, 5.0).astype(jnp.bfloat16)


def draw_selected(key, part):
    key = jax.random.fold_in(key, 5)
    popular_key = jax.random.fold_in(key, 1)
    noise_key = jax.random.fold_in(key, 2)
    popular = (jax.random.randint(popular_key, (NB,), 0, 4) == 0).astype(jnp.int32)
    noise = jax.random.randint(noise_key, (NB, NB), 0, 2048)
    rows_at = jnp.arange(NB, dtype=jnp.int32)[:, None]
    cols_at = jnp.arange(NB, dtype=jnp.int32)[None, :]
    base = noise + popular[None, :] * 1536
    base = jnp.where(cols_at == rows_at - 1, 8192, base)
    ranked = jnp.where(cols_at < rows_at, base * NB + cols_at, -1 - cols_at)
    picks = lax.top_k(ranked, TOPK)[1].astype(jnp.int32)
    return jnp.where(picks < rows_at, picks, rows_at).astype(jnp.int32)


def level_of(rng, shape, pieces, smallest, top_value):
    def one(axis_at, blocks):
        draws = jax.random.uniform(jax.random.fold_in(jax.random.fold_in(rng, 6), axis_at), (blocks,), jnp.float32, smallest / len(pieces), top_value / len(pieces))
        return jnp.repeat(jnp.exp(draws), shape[axis_at] // blocks).reshape((-1,) + (1,) * (len(shape) - axis_at - 1))

    factor_of = one(*pieces[0])
    for cut in pieces[1:]:
        factor_of = factor_of * one(*cut)
    return factor_of


def gaussian(own_key, extent, scale, limit, split=(), held_as=jnp.bfloat16):
    drawn = jax.random.normal(own_key, extent, jnp.float32) * scale
    if len(split) > 0:
        drawn = level_of(own_key, extent, split, -0.22, 0.18) * drawn
    return jnp.clip(drawn, min=-limit, max=limit).astype(held_as)


def setup_inputs(seed: int = 0) -> dict:
    arg_keys = jax.random.split(jax.random.key(seed), 5)
    return {
        "queries": draw_queries(jax.random.fold_in(arg_keys[4], 71), 0),
        "keys": draw_keys(jax.random.fold_in(arg_keys[4], 71), 0),
        "values": gaussian(arg_keys[2], (TOKENS, HEADS, HEAD_DIM), 1.0, 6.0, ((0, 64), (1, 8))),
        "selected": draw_selected(jax.random.fold_in(arg_keys[4], 71), 0),
    }


masked_fill = -1.0e30


def attend_one(query_block, own_keys, own_values, far_keys, far_values, live_slots):
    span = (TOPK + 1) * BLOCK
    all_keys = jnp.concatenate([own_keys[None], far_keys], 0).reshape(span, HEADS, HEAD_DIM)
    all_values = jnp.concatenate([own_values[None], far_values], 0).reshape(span, HEADS, HEAD_DIM)
    score_scale = HEAD_DIM ** -0.5
    scores = jnp.einsum("qhd,khd->hqk", query_block.astype(jnp.float32), all_keys.astype(jnp.float32)) * score_scale
    rows_pos = jnp.arange(BLOCK, dtype=jnp.int32)[:, None]
    cols_pos = jnp.arange(span, dtype=jnp.int32)[None, :]
    slot_of = cols_pos // BLOCK
    in_block = cols_pos % BLOCK
    live_full = jnp.concatenate([jnp.ones((1,), dtype=bool), live_slots], 0)
    live_cols = jnp.take(live_full, slot_of)
    allowed = ((slot_of == 0) & (in_block <= rows_pos)) | ((slot_of > 0) & live_cols)
    scores = jnp.where(allowed[None], scores, masked_fill)
    row_max = jnp.max(scores, axis=2, keepdims=True)
    weights = jnp.where(allowed[None], jnp.exp(scores - row_max), 0.0)
    totals = jnp.sum(weights, axis=2)
    rounded = weights.astype(jnp.bfloat16)
    mixed = jnp.einsum("hqk,khd->qhd", rounded.astype(jnp.float32), all_values.astype(jnp.float32))
    return (mixed / totals.T[:, :, None]).astype(jnp.bfloat16)


def reference(queries, keys, values, selected):
    query_blocks = queries.reshape(NB, BLOCK, HEADS, HEAD_DIM)
    key_blocks = keys.reshape(NB, BLOCK, HEADS, HEAD_DIM)
    value_blocks = values.reshape(NB, BLOCK, HEADS, HEAD_DIM)

    def one_block(block_at):
        picks = selected[block_at].astype(jnp.int32)
        return attend_one(query_blocks[block_at], key_blocks[block_at], value_blocks[block_at],
                          key_blocks[picks], value_blocks[picks], picks != block_at)

    attended = lax.map(one_block, jnp.arange(NB, dtype=jnp.int32))
    return attended.reshape(TOKENS, HEADS * HEAD_DIM)
```

```python
import functools
import math

import jax
import jax.numpy as jnp
from jax import lax
from jax.experimental import pallas as pl
from jax.experimental.pallas import tpu as pltpu
from jax.sharding import PartitionSpec as P

HEAD_DIM = 128
BLOCK = 256
CHUNKS = 2
MESH = pl.DeviceIdType.MESH
STRIDE = 27

FILL = -1e30
EXP_SCALE = HEAD_DIM ** (-0.5) * math.log2(math.e)


def kernel(
    n_ctx, n_head, heads,
    sel_ref, q_hbm, k_hbm, v_hbm, out_ref,
    q_ref, k_ref, v_ref, in_sem, q_heads, own, send, far, near, staged, wide,
    sel_own, sel_all, sel_smem,
    sel_send, sel_recv, sel_local, spread_send, spread_recv, fetch_send, fetch_recv,
    near_send, near_recv, out_send, out_recv,
    *spread,
):
    group = heads // CHUNKS
    pieces_of_head = n_ctx // (2 * group)
    me = lax.axis_index("ctx")
    my_head = lax.axis_index("head")
    right = lax.rem(me + 1, n_ctx)
    rows_out = BLOCK // n_head
    cols_out = group * HEAD_DIM

    def to_ctx(i):
        return lax.rem(me + i * STRIDE, n_ctx)

    def to_head(i):
        return lax.rem(my_head + i, n_head)

    loads = [
        pltpu.make_async_copy(src, dst, in_sem.at[i])
        for i, (src, dst) in enumerate([(k_hbm, k_ref), (v_hbm, v_ref), (q_hbm, q_ref)])
    ]
    for load in loads:
        load.start()

    barrier = pltpu.get_barrier_semaphore()

    @pl.loop(1, n_ctx)
    def _(i):
        pl.semaphore_signal(barrier, inc=1, device_id={"ctx": to_ctx(i)}, device_id_type=MESH)

    @pl.loop(1, n_head)
    def _(i):
        pl.semaphore_signal(barrier, inc=1, device_id={"head": to_head(i)}, device_id_type=MESH)

    s0, s1, s2 = sel_ref[0, 0], sel_ref[0, 1], sel_ref[0, 2]
    far_a = jnp.where(s0 == me - 1, s1, s0)
    far_b = jnp.where(s2 == me - 1, s1, s2)
    lane = lax.broadcasted_iota(jnp.int32, (1, 128), 1)
    sel_own[...] = jnp.where(lane == 0, far_a, far_b)

    def split_heads(src, store, first, count):
        wide[...] = src[...].astype(jnp.float32).reshape(BLOCK * heads, HEAD_DIM)
        for h in range(first, first + count):
            store(h, wide[pl.ds(h, BLOCK, stride=heads), :].astype(jnp.bfloat16))

    def store_own(kind):
        def store(h, rows):
            chunk, at = divmod(h, group)
            start = (kind * group + at) * pieces_of_head
            own[chunk, pl.ds(start, pieces_of_head)] = rows.reshape(
                pieces_of_head, BLOCK // pieces_of_head, HEAD_DIM
            )
        return store

    def store_q(h, rows):
        q_heads[h] = rows

    def spread_copy(chunk, peer):
        return pltpu.make_async_remote_copy(
            src_ref=own.at[chunk, peer], dst_ref=spread[chunk].at[me],
            send_sem=spread_send.at[chunk], recv_sem=spread_recv.at[chunk],
            device_id={"ctx": peer}, device_id_type=MESH,
        )

    def near_copy(chunk):
        return pltpu.make_async_remote_copy(
            src_ref=own.at[chunk], dst_ref=near.at[chunk],
            send_sem=near_send.at[chunk], recv_sem=near_recv.at[chunk],
            device_id={"ctx": right}, device_id_type=MESH,
        )

    def sel_copy(peer):
        return pltpu.make_async_remote_copy(
            src_ref=sel_own, dst_ref=sel_all.at[me],
            send_sem=sel_send, recv_sem=sel_recv,
            device_id={"ctx": peer}, device_id_type=MESH,
        )

    def fetch_copy(chunk, peer):
        return pltpu.make_async_remote_copy(
            src_ref=send.at[chunk, peer], dst_ref=far.at[chunk, :, me],
            send_sem=fetch_send.at[chunk], recv_sem=fetch_recv.at[chunk],
            device_id={"ctx": peer}, device_id_type=MESH,
        )

    def out_slot(chunk):
        return out_ref.at[:, pl.ds(pl.multiple_of(my_head * (heads * HEAD_DIM) + chunk * cols_out, HEAD_DIM), cols_out)]

    def out_copy(chunk, peer):
        return pltpu.make_async_remote_copy(
            src_ref=staged.at[chunk, peer], dst_ref=out_slot(chunk),
            send_sem=out_send.at[chunk], recv_sem=out_recv.at[chunk],
            device_id={"head": peer}, device_id_type=MESH,
        )

    def wait_bytes(ref, sem):
        pltpu.make_async_copy(ref, ref, sem).wait()

    loads[0].wait()
    split_heads(k_ref, store_own(0), 0, heads)
    loads[1].wait()
    split_heads(v_ref, store_own(1), 0, heads)

    pl.semaphore_wait(barrier, n_ctx - 1 + n_head - 1)

    pltpu.make_async_copy(sel_own, sel_all.at[me], sel_recv).start()

    @pl.loop(1, n_ctx)
    def _(i):
        sel_copy(to_ctx(i)).start()

    for chunk in range(CHUNKS):
        pltpu.make_async_copy(own.at[chunk, me], spread[chunk].at[me], spread_recv.at[chunk]).start()

        @pl.loop(1, n_ctx)
        def _(i):
            spread_copy(chunk, to_ctx(i)).start()

        near_copy(chunk).start()

    loads[2].wait()
    split_heads(q_ref, store_q, 0, heads)

    wait_bytes(sel_all, sel_recv)
    sel_down = pltpu.make_async_copy(sel_all, sel_smem, sel_local)
    sel_down.start()
    sel_down.wait()

    for chunk in range(CHUNKS):
        wait_bytes(spread[chunk], spread_recv.at[chunk])

        def fill(peer):
            for slot in range(2):
                send[chunk, peer, slot] = spread[chunk][sel_smem[peer, 0, slot]]

        @pl.loop(1, n_ctx)
        def _(i):
            peer = to_ctx(i)
            fill(peer)
            fetch_copy(chunk, peer).start()

        fill(me)
        pltpu.make_async_copy(send.at[chunk, me], far.at[chunk, :, me], fetch_recv.at[chunk]).start()

    causal = lax.broadcasted_iota(jnp.int32, (BLOCK, BLOCK), 1) <= lax.broadcasted_iota(
        jnp.int32, (BLOCK, BLOCK), 0
    )
    near_live, a_live, b_live = me >= 1, far_a != me, far_b != me

    def scores(q, k):
        return lax.dot_general(q, k, (((1,), (1,)), ((), ())), preferred_element_type=jnp.float32)

    def half_max(s):
        return jnp.maximum(s[:, :128], s[:, 128:])

    for chunk in range(CHUNKS):
        wait_bytes(near.at[chunk], near_recv.at[chunk])
        wait_bytes(far.at[chunk], fetch_recv.at[chunk])

        for at in range(group):
            def pick(buf, kind):
                first = (kind * group + at) * pieces_of_head
                return buf[pl.ds(first, pieces_of_head)].reshape(BLOCK, HEAD_DIM)

            blocks = [own.at[chunk], near.at[chunk], far.at[chunk, 0], far.at[chunk, 1]]
            live = [None, near_live, a_live, b_live]
            q = q_heads[chunk * group + at]
            s = [scores(q, pick(b, 0)) for b in blocks]
            s[0] = jnp.where(causal, s[0], FILL)
            top = half_max(s[0])
            for one, ok in zip(s[1:], live[1:]):
                top = jnp.maximum(top, jnp.where(ok, half_max(one), FILL))
            top = jnp.max(top, axis=1, keepdims=True) * EXP_SCALE
            total, mixed = None, None
            for one, ok, b in zip(s, live, blocks):
                shift = top if ok is None else jnp.where(ok, top, -FILL)
                w = jnp.exp2(one * EXP_SCALE - shift)
                part = w[:, :128] + w[:, 128:]
                total = part if total is None else total + part
                part = jnp.dot(w.astype(jnp.bfloat16), pick(b, 1), preferred_element_type=jnp.float32)
                mixed = part if mixed is None else mixed + part
            total = jnp.sum(total, axis=1, keepdims=True)
            rows = (mixed / total).astype(jnp.bfloat16)
            staged[chunk, :, :, at * HEAD_DIM : (at + 1) * HEAD_DIM] = rows.reshape(
                n_head, rows_out, HEAD_DIM
            )

        pltpu.make_async_copy(staged.at[chunk, my_head], out_slot(chunk), out_recv.at[chunk]).start()

        @pl.loop(1, n_head)
        def _(i):
            out_copy(chunk, to_head(i)).start()

    others = pl.ds(0, n_ctx - 1)
    wait_bytes(sel_all.at[others], sel_send)
    for chunk in range(CHUNKS):
        wait_bytes(spread[chunk].at[others], spread_send.at[chunk])
        wait_bytes(send.at[chunk, others], fetch_send.at[chunk])
        wait_bytes(near.at[chunk], near_send.at[chunk])
        wait_bytes(staged.at[chunk, pl.ds(0, n_head - 1)], out_send.at[chunk])
        wait_bytes(staged.at[chunk], out_recv.at[chunk])


def on_device(n_ctx, n_head, selected, queries, keys, values):
    heads = queries.shape[1]
    group = heads // CHUNKS
    piece = 2 * group * BLOCK // n_ctx
    bf16, dma = jnp.bfloat16, pltpu.SemaphoreType.DMA
    hbm = pl.BlockSpec(memory_space=pltpu.HBM)
    return pl.pallas_call(
        functools.partial(kernel, n_ctx, n_head, heads),
        out_shape=jax.ShapeDtypeStruct((BLOCK // n_head, n_head * heads * HEAD_DIM), bf16),
        in_specs=[pl.BlockSpec(memory_space=pltpu.SMEM), hbm, hbm, hbm],
        out_specs=pl.BlockSpec(memory_space=pl.ANY),
        scratch_shapes=[
            *[pltpu.VMEM((BLOCK, heads, HEAD_DIM), bf16)] * 3,
            dma((3,)),
            pltpu.VMEM((heads, BLOCK, HEAD_DIM), bf16),
            pltpu.VMEM((CHUNKS, n_ctx, piece, HEAD_DIM), bf16),
            pltpu.VMEM((CHUNKS, n_ctx, 2, piece, HEAD_DIM), bf16),
            pltpu.VMEM((CHUNKS, 2, n_ctx, piece, HEAD_DIM), bf16),
            pltpu.VMEM((CHUNKS, n_ctx, piece, HEAD_DIM), bf16),
            pltpu.VMEM((CHUNKS, n_head, BLOCK // n_head, group * HEAD_DIM), bf16),
            pltpu.VMEM((BLOCK * heads, HEAD_DIM), jnp.float32),
            pltpu.VMEM((1, 128), jnp.int32),
            pltpu.VMEM((n_ctx, 1, 128), jnp.int32),
            pltpu.SMEM((n_ctx, 1, 128), jnp.int32),
            dma, dma, dma,
            dma((CHUNKS,)), dma((CHUNKS,)),
            dma((CHUNKS,)), dma((CHUNKS,)),
            dma((CHUNKS,)), dma((CHUNKS,)),
            dma((CHUNKS,)), dma((CHUNKS,)),
            *[pltpu.VMEM((n_ctx, piece, HEAD_DIM), bf16)] * CHUNKS,
        ],
        compiler_params=pltpu.CompilerParams(
            collective_id=0, has_side_effects=True, vmem_limit_bytes=63 * 1024 * 1024
        ),
        name="moba",
    )(selected, queries, keys, values)


def solution(mesh):
    n_ctx, n_head = mesh.shape["ctx"], mesh.shape["head"]

    def run(queries, keys, values, selected):
        return on_device(n_ctx, n_head, selected, queries, keys, values)

    return jax.shard_map(
        run,
        mesh=mesh,
        in_specs=(
            P("ctx", "head", None),
            P("ctx", "head", None),
            P("ctx", "head", None),
            P("ctx", None),
        ),
        out_specs=P(("ctx", "head"), None),
        check_vma=False,
    )
```

```python
import functools
import math

import jax
import jax.numpy as jnp
from jax import lax
from jax.experimental import pallas as pl
from jax.experimental.pallas import tpu as pltpu
from jax.sharding import PartitionSpec as P

HEAD_DIM = 128
BLOCK = 256
CHUNKS = 4
QUERIES_AFTER = 1
ATTEND_AFTER = 1
MESH = pl.DeviceIdType.MESH
STRIDE = 27

FILL = -1e30
EXP_SCALE = HEAD_DIM ** (-0.5) * math.log2(math.e)


def kernel(
    n_ctx, n_head, heads,
    sel_ref, q_hbm, k_hbm, v_hbm, out_ref,
    q_ref, k_ref, v_ref, in_sem, q_heads, own, send, far, staged, wide,
    q_next, part, part_back, stats, stats_back,
    sel_own, sel_all, sel_smem,
    sel_send, sel_recv, sel_local, spread_send, spread_recv, fetch_send, fetch_recv,
    back_send, back_recv, out_send, out_recv,
    *spread,
):
    group = heads // CHUNKS
    pieces_of_head = n_ctx // (2 * group)
    me = lax.axis_index("ctx")
    my_head = lax.axis_index("head")
    right, left = lax.rem(me + 1, n_ctx), lax.rem(me + n_ctx - 1, n_ctx)
    rows_out = BLOCK // n_head
    cols_out = group * HEAD_DIM

    def to_ctx(i):
        return lax.rem(me + i * STRIDE, n_ctx)

    def to_head(i):
        return lax.rem(my_head + i, n_head)

    loads = [
        pltpu.make_async_copy(src, dst, in_sem.at[i])
        for i, (src, dst) in enumerate([(k_hbm, k_ref), (v_hbm, v_ref), (q_hbm, q_ref)])
    ]
    for load in loads:
        load.start()

    barrier = pltpu.get_barrier_semaphore()

    @pl.loop(1, n_ctx)
    def _(i):
        pl.semaphore_signal(barrier, inc=1, device_id={"ctx": to_ctx(i)}, device_id_type=MESH)

    @pl.loop(1, n_head)
    def _(i):
        pl.semaphore_signal(barrier, inc=1, device_id={"head": to_head(i)}, device_id_type=MESH)

    s0, s1, s2 = sel_ref[0, 0], sel_ref[0, 1], sel_ref[0, 2]
    far_a = jnp.where(s0 == me - 1, s1, s0)
    far_b = jnp.where(s2 == me - 1, s1, s2)
    lane = lax.broadcasted_iota(jnp.int32, (1, 128), 1)
    sel_own[...] = jnp.where(lane == 0, far_a, far_b)

    def split_heads(src, store, first, count):
        wide[...] = src[...].astype(jnp.float32).reshape(BLOCK * heads, HEAD_DIM)
        for h in range(first, first + count):
            store(h, wide[pl.ds(h, BLOCK, stride=heads), :].astype(jnp.bfloat16))

    def store_own(kind):
        def store(h, rows):
            chunk, at = divmod(h, group)
            start = (kind * group + at) * pieces_of_head
            own[chunk, pl.ds(start, pieces_of_head)] = rows.reshape(
                pieces_of_head, BLOCK // pieces_of_head, HEAD_DIM
            )
        return store

    def store_q(h, rows):
        q_heads[h] = rows

    def spread_copy(chunk, peer):
        return pltpu.make_async_remote_copy(
            src_ref=own.at[chunk, peer], dst_ref=spread[chunk].at[me],
            send_sem=spread_send.at[chunk], recv_sem=spread_recv.at[chunk],
            device_id={"ctx": peer}, device_id_type=MESH,
        )

    def pass_copy(at, src, dst, peer):
        return pltpu.make_async_remote_copy(
            src_ref=src, dst_ref=dst, send_sem=back_send.at[at], recv_sem=back_recv.at[at],
            device_id={"ctx": peer}, device_id_type=MESH,
        )

    query_copy = pass_copy(0, q_heads, q_next, left)
    part_copy = pass_copy(1, part, part_back, right)
    stats_copy = pass_copy(2, stats, stats_back, right)

    def sel_copy(peer):
        return pltpu.make_async_remote_copy(
            src_ref=sel_own, dst_ref=sel_all.at[me],
            send_sem=sel_send, recv_sem=sel_recv,
            device_id={"ctx": peer}, device_id_type=MESH,
        )

    def fetch_copy(chunk, peer):
        return pltpu.make_async_remote_copy(
            src_ref=send.at[chunk, peer], dst_ref=far.at[chunk, :, me],
            send_sem=fetch_send.at[chunk], recv_sem=fetch_recv.at[chunk],
            device_id={"ctx": peer}, device_id_type=MESH,
        )

    def out_slot(chunk):
        return out_ref.at[:, pl.ds(pl.multiple_of(my_head * (heads * HEAD_DIM) + chunk * cols_out, HEAD_DIM), cols_out)]

    def out_copy(chunk, peer):
        return pltpu.make_async_remote_copy(
            src_ref=staged.at[chunk, peer], dst_ref=out_slot(chunk),
            send_sem=out_send.at[chunk], recv_sem=out_recv.at[chunk],
            device_id={"head": peer}, device_id_type=MESH,
        )

    def wait_bytes(ref, sem):
        pltpu.make_async_copy(ref, ref, sem).wait()

    loads[0].wait()
    split_heads(k_ref, store_own(0), 0, heads)
    loads[1].wait()
    split_heads(v_ref, store_own(1), 0, heads)

    loads[2].wait()
    split_heads(q_ref, store_q, 0, heads)

    pl.semaphore_wait(barrier, n_ctx - 1 + n_head - 1)

    pltpu.make_async_copy(sel_own, sel_all.at[me], sel_recv).start()

    @pl.loop(1, n_ctx)
    def _(i):
        sel_copy(to_ctx(i)).start()

    for chunk in range(CHUNKS):
        pltpu.make_async_copy(own.at[chunk, me], spread[chunk].at[me], spread_recv.at[chunk]).start()

        @pl.loop(1, n_ctx)
        def _(i):
            spread_copy(chunk, to_ctx(i)).start()

        if chunk == QUERIES_AFTER:
            query_copy.start()


    wait_bytes(sel_all, sel_recv)
    sel_down = pltpu.make_async_copy(sel_all, sel_smem, sel_local)
    sel_down.start()
    sel_down.wait()

    causal = lax.broadcasted_iota(jnp.int32, (BLOCK, BLOCK), 1) <= lax.broadcasted_iota(
        jnp.int32, (BLOCK, BLOCK), 0
    )
    near_live, a_live, b_live = me >= 1, far_a != me, far_b != me
    stat_lane = lax.broadcasted_iota(jnp.int32, (BLOCK, 128), 1)

    def scores(q, k):
        return lax.dot_general(q, k, (((1,), (1,)), ((), ())), preferred_element_type=jnp.float32)

    def half_max(s):
        return jnp.maximum(s[:, :128], s[:, 128:])

    def pick(buf, kind, at):
        first = (kind * group + at) * pieces_of_head
        return buf[pl.ds(first, pieces_of_head)].reshape(BLOCK, HEAD_DIM)

    def attend_next():
        columns = jnp.zeros((BLOCK, 128), jnp.float32)
        for h in range(heads):
            chunk, at = divmod(h, group)
            s = scores(q_next[h], pick(own.at[chunk], 0, at))
            top = jnp.max(half_max(s), axis=1, keepdims=True) * EXP_SCALE
            w = jnp.exp2(s * EXP_SCALE - top)
            total = jnp.sum(w[:, :128] + w[:, 128:], axis=1, keepdims=True)
            mixed = jnp.dot(
                w.astype(jnp.bfloat16), pick(own.at[chunk], 1, at), preferred_element_type=jnp.float32
            )
            part[h] = (mixed / total).astype(jnp.bfloat16)
            columns = jnp.where(stat_lane == 2 * h, top, columns)
            columns = jnp.where(stat_lane == 2 * h + 1, total, columns)
        stats[...] = columns.T[: 2 * heads]

    for chunk in range(CHUNKS):
        wait_bytes(spread[chunk], spread_recv.at[chunk])

        def fill(peer):
            for slot in range(2):
                send[chunk, peer, slot] = spread[chunk][sel_smem[peer, 0, slot]]

        @pl.loop(1, n_ctx)
        def _(i):
            peer = to_ctx(i)
            fill(peer)
            fetch_copy(chunk, peer).start()

        fill(me)
        pltpu.make_async_copy(send.at[chunk, me], far.at[chunk, :, me], fetch_recv.at[chunk]).start()

        if chunk == ATTEND_AFTER:
            query_copy.wait_recv()
            attend_next()
            part_copy.start()
            stats_copy.start()

    part_copy.wait_recv()
    stats_copy.wait_recv()
    columns = jnp.concatenate(
        [stats_back[...], jnp.zeros((128 - 2 * heads, BLOCK), jnp.float32)], 0
    ).T

    for chunk in range(CHUNKS):
        wait_bytes(far.at[chunk], fetch_recv.at[chunk])

        for at in range(group):
            blocks = [own.at[chunk], far.at[chunk, 0], far.at[chunk, 1]]
            live = [None, a_live, b_live]
            h = chunk * group + at
            s = [scores(q_heads[h], pick(b, 0, at)) for b in blocks]
            s[0] = jnp.where(causal, s[0], FILL)
            top = half_max(s[0])
            for one, ok in zip(s[1:], live[1:]):
                top = jnp.maximum(top, jnp.where(ok, half_max(one), FILL))
            near_top = jnp.where(near_live, columns[:, 2 * h : 2 * h + 1], FILL)
            top = jnp.maximum(jnp.max(top, axis=1, keepdims=True) * EXP_SCALE, near_top)
            total, mixed = None, None
            for one, ok, b in zip(s, live, blocks):
                shift = top if ok is None else jnp.where(ok, top, -FILL)
                w = jnp.exp2(one * EXP_SCALE - shift)
                part = w[:, :128] + w[:, 128:]
                total = part if total is None else total + part
                part = jnp.dot(w.astype(jnp.bfloat16), pick(b, 1, at), preferred_element_type=jnp.float32)
                mixed = part if mixed is None else mixed + part
            near_total = jnp.exp2(near_top - top) * columns[:, 2 * h + 1 : 2 * h + 2]
            total = jnp.sum(total, axis=1, keepdims=True) + near_total
            mixed = mixed + part_back[h].astype(jnp.float32) * near_total
            rows = (mixed / total).astype(jnp.bfloat16)
            staged[chunk, :, :, at * HEAD_DIM : (at + 1) * HEAD_DIM] = rows.reshape(
                n_head, rows_out, HEAD_DIM
            )

        pltpu.make_async_copy(staged.at[chunk, my_head], out_slot(chunk), out_recv.at[chunk]).start()

        @pl.loop(1, n_head)
        def _(i):
            out_copy(chunk, to_head(i)).start()

    others = pl.ds(0, n_ctx - 1)
    wait_bytes(sel_all.at[others], sel_send)
    query_copy.wait_send()
    part_copy.wait_send()
    stats_copy.wait_send()
    for chunk in range(CHUNKS):
        wait_bytes(spread[chunk].at[others], spread_send.at[chunk])
        wait_bytes(send.at[chunk, others], fetch_send.at[chunk])
        wait_bytes(staged.at[chunk, pl.ds(0, n_head - 1)], out_send.at[chunk])
        wait_bytes(staged.at[chunk], out_recv.at[chunk])


def on_device(n_ctx, n_head, selected, queries, keys, values):
    heads = queries.shape[1]
    group = heads // CHUNKS
    piece = 2 * group * BLOCK // n_ctx
    bf16, dma = jnp.bfloat16, pltpu.SemaphoreType.DMA
    hbm = pl.BlockSpec(memory_space=pltpu.HBM)
    return pl.pallas_call(
        functools.partial(kernel, n_ctx, n_head, heads),
        out_shape=jax.ShapeDtypeStruct((BLOCK // n_head, n_head * heads * HEAD_DIM), bf16),
        in_specs=[pl.BlockSpec(memory_space=pltpu.SMEM), hbm, hbm, hbm],
        out_specs=pl.BlockSpec(memory_space=pl.ANY),
        scratch_shapes=[
            *[pltpu.VMEM((BLOCK, heads, HEAD_DIM), bf16)] * 3,
            dma((3,)),
            pltpu.VMEM((heads, BLOCK, HEAD_DIM), bf16),
            pltpu.VMEM((CHUNKS, n_ctx, piece, HEAD_DIM), bf16),
            pltpu.VMEM((CHUNKS, n_ctx, 2, piece, HEAD_DIM), bf16),
            pltpu.VMEM((CHUNKS, 2, n_ctx, piece, HEAD_DIM), bf16),
            pltpu.VMEM((CHUNKS, n_head, BLOCK // n_head, group * HEAD_DIM), bf16),
            pltpu.VMEM((BLOCK * heads, HEAD_DIM), jnp.float32),
            *[pltpu.VMEM((heads, BLOCK, HEAD_DIM), bf16)] * 3,
            *[pltpu.VMEM((2 * heads, BLOCK), jnp.float32)] * 2,
            pltpu.VMEM((1, 128), jnp.int32),
            pltpu.VMEM((n_ctx, 1, 128), jnp.int32),
            pltpu.SMEM((n_ctx, 1, 128), jnp.int32),
            dma, dma, dma,
            dma((CHUNKS,)), dma((CHUNKS,)),
            dma((CHUNKS,)), dma((CHUNKS,)),
            dma((3,)), dma((3,)),
            dma((CHUNKS,)), dma((CHUNKS,)),
            *[pltpu.VMEM((n_ctx, piece, HEAD_DIM), bf16)] * CHUNKS,
        ],
        compiler_params=pltpu.CompilerParams(
            collective_id=0, has_side_effects=True, vmem_limit_bytes=63 * 1024 * 1024
        ),
        name="moba",
    )(selected, queries, keys, values)


def solution(mesh):
    n_ctx, n_head = mesh.shape["ctx"], mesh.shape["head"]

    def run(queries, keys, values, selected):
        return on_device(n_ctx, n_head, selected, queries, keys, values)

    return jax.shard_map(
        run,
        mesh=mesh,
        in_specs=(
            P("ctx", "head", None),
            P("ctx", "head", None),
            P("ctx", "head", None),
            P("ctx", None),
        ),
        out_specs=P(("ctx", "head"), None),
        check_vma=False,
    )
```

```python
import functools
import math

import jax
import jax.numpy as jnp
from jax import lax
from jax.experimental import pallas as pl
from jax.experimental.pallas import tpu as pltpu
from jax.sharding import PartitionSpec as P

HEAD_DIM = 128
BLOCK = 256
CHUNKS = 4
QUERIES_AFTER = 1
ATTEND_AFTER = 1
MESH = pl.DeviceIdType.MESH
STRIDE = 27

FILL = -1e30
EXP_SCALE = HEAD_DIM ** (-0.5) * math.log2(math.e)


def kernel(
    n_ctx, n_head, heads,
    sel_ref, q_hbm, k_hbm, v_hbm, out_ref,
    q_ref, k_ref, v_ref, in_sem, q_heads, own, send, far, staged, wide,
    q_next, part, part_back, stats, stats_back,
    sel_own, sel_all, sel_smem,
    sel_send, sel_recv, sel_local, spread_send, spread_recv, fetch_send, fetch_recv,
    back_send, back_recv, out_send, out_recv,
    *spread,
):
    group = heads // CHUNKS
    pieces_of_head = n_ctx // (2 * group)
    me = lax.axis_index("ctx")
    my_head = lax.axis_index("head")
    right, left = lax.rem(me + 1, n_ctx), lax.rem(me + n_ctx - 1, n_ctx)
    rows_out = BLOCK // n_head
    cols_out = group * HEAD_DIM

    def to_ctx(i):
        return lax.rem(me + i * STRIDE, n_ctx)

    def to_head(i):
        return lax.rem(my_head + i, n_head)

    loads = [
        pltpu.make_async_copy(src, dst, in_sem.at[i])
        for i, (src, dst) in enumerate([(k_hbm, k_ref), (v_hbm, v_ref), (q_hbm, q_ref)])
    ]
    for load in loads:
        load.start()

    barrier = pltpu.get_barrier_semaphore()

    @pl.loop(1, n_ctx)
    def _(i):
        pl.semaphore_signal(barrier, inc=1, device_id={"ctx": to_ctx(i)}, device_id_type=MESH)

    @pl.loop(1, n_head)
    def _(i):
        pl.semaphore_signal(barrier, inc=1, device_id={"head": to_head(i)}, device_id_type=MESH)

    s0, s1, s2 = sel_ref[0, 0], sel_ref[0, 1], sel_ref[0, 2]
    far_a = jnp.where(s0 == me - 1, s1, s0)
    far_b = jnp.where(s2 == me - 1, s1, s2)
    lane = lax.broadcasted_iota(jnp.int32, (1, 128), 1)
    sel_own[...] = jnp.where(lane == 0, far_a, far_b)

    def split_heads(src, store, first, count):
        wide[...] = src[...].astype(jnp.float32).reshape(BLOCK * heads, HEAD_DIM)
        for h in range(first, first + count):
            store(h, wide[pl.ds(h, BLOCK, stride=heads), :].astype(jnp.bfloat16))

    def store_own(kind):
        def store(h, rows):
            chunk, at = divmod(h, group)
            start = (kind * group + at) * pieces_of_head
            own[chunk, pl.ds(start, pieces_of_head)] = rows.reshape(
                pieces_of_head, BLOCK // pieces_of_head, HEAD_DIM
            )
        return store

    def store_q(h, rows):
        q_heads[h] = rows

    def spread_copy(chunk, peer):
        return pltpu.make_async_remote_copy(
            src_ref=own.at[chunk, peer], dst_ref=spread[chunk].at[me],
            send_sem=spread_send.at[chunk], recv_sem=spread_recv.at[chunk],
            device_id={"ctx": peer}, device_id_type=MESH,
        )

    def pass_copy(at, src, dst, peer):
        return pltpu.make_async_remote_copy(
            src_ref=src, dst_ref=dst, send_sem=back_send.at[at], recv_sem=back_recv.at[at],
            device_id={"ctx": peer}, device_id_type=MESH,
        )

    query_copy = pass_copy(0, q_heads, q_next, left)
    part_copy = pass_copy(1, part, part_back, right)
    stats_copy = pass_copy(2, stats, stats_back, right)

    def sel_copy(peer):
        return pltpu.make_async_remote_copy(
            src_ref=sel_own, dst_ref=sel_all.at[me],
            send_sem=sel_send, recv_sem=sel_recv,
            device_id={"ctx": peer}, device_id_type=MESH,
        )

    def fetch_copy(chunk, peer):
        return pltpu.make_async_remote_copy(
            src_ref=send.at[chunk, peer], dst_ref=far.at[chunk, :, me],
            send_sem=fetch_send.at[chunk], recv_sem=fetch_recv.at[chunk],
            device_id={"ctx": peer}, device_id_type=MESH,
        )

    def out_slot(chunk):
        return out_ref.at[:, pl.ds(pl.multiple_of(my_head * (heads * HEAD_DIM) + chunk * cols_out, HEAD_DIM), cols_out)]

    def out_copy(chunk, peer):
        return pltpu.make_async_remote_copy(
            src_ref=staged.at[chunk, peer], dst_ref=out_slot(chunk),
            send_sem=out_send.at[chunk], recv_sem=out_recv.at[chunk],
            device_id={"head": peer}, device_id_type=MESH,
        )

    def wait_bytes(ref, sem):
        pltpu.make_async_copy(ref, ref, sem).wait()

    loads[0].wait()
    split_heads(k_ref, store_own(0), 0, heads)
    loads[1].wait()
    split_heads(v_ref, store_own(1), 0, heads)

    loads[2].wait()
    split_heads(q_ref, store_q, 0, heads)

    pl.semaphore_wait(barrier, n_ctx - 1 + n_head - 1)

    pltpu.make_async_copy(sel_own, sel_all.at[me], sel_recv).start()

    for chunk in range(CHUNKS):
        pltpu.make_async_copy(own.at[chunk, me], spread[chunk].at[me], spread_recv.at[chunk]).start()

        @pl.loop(1, n_ctx)
        def _(i):
            spread_copy(chunk, to_ctx(i)).start()

        if chunk == 0:
            @pl.loop(1, n_ctx)
            def _(i):
                sel_copy(to_ctx(i)).start()

        if chunk == QUERIES_AFTER:
            query_copy.start()


    wait_bytes(sel_all, sel_recv)
    sel_down = pltpu.make_async_copy(sel_all, sel_smem, sel_local)
    sel_down.start()
    sel_down.wait()

    causal = lax.broadcasted_iota(jnp.int32, (BLOCK, BLOCK), 1) <= lax.broadcasted_iota(
        jnp.int32, (BLOCK, BLOCK), 0
    )
    near_live, a_live, b_live = me >= 1, far_a != me, far_b != me
    stat_lane = lax.broadcasted_iota(jnp.int32, (BLOCK, 128), 1)

    def scores(q, k):
        return lax.dot_general(q, k, (((1,), (1,)), ((), ())), preferred_element_type=jnp.float32)

    def half_max(s):
        return jnp.maximum(s[:, :128], s[:, 128:])

    def pick(buf, kind, at):
        first = (kind * group + at) * pieces_of_head
        return buf[pl.ds(first, pieces_of_head)].reshape(BLOCK, HEAD_DIM)

    def attend_next():
        columns = jnp.zeros((BLOCK, 128), jnp.float32)
        for h in range(heads):
            chunk, at = divmod(h, group)
            s = scores(q_next[h], pick(own.at[chunk], 0, at))
            top = jnp.max(half_max(s), axis=1, keepdims=True) * EXP_SCALE
            w = jnp.exp2(s * EXP_SCALE - top)
            total = jnp.sum(w[:, :128] + w[:, 128:], axis=1, keepdims=True)
            mixed = jnp.dot(
                w.astype(jnp.bfloat16), pick(own.at[chunk], 1, at), preferred_element_type=jnp.float32
            )
            part[h] = (mixed / total).astype(jnp.bfloat16)
            columns = jnp.where(stat_lane == 2 * h, top, columns)
            columns = jnp.where(stat_lane == 2 * h + 1, total, columns)
        stats[...] = columns.T[: 2 * heads]

    for chunk in range(CHUNKS):
        wait_bytes(spread[chunk], spread_recv.at[chunk])

        @pl.loop(0, n_ctx, unroll=8)
        def _(peer):
            for slot in range(2):
                send[chunk, peer, slot] = spread[chunk][sel_smem[peer, 0, slot]]

        @pl.loop(1, n_ctx)
        def _(i):
            fetch_copy(chunk, to_ctx(i)).start()

        pltpu.make_async_copy(send.at[chunk, me], far.at[chunk, :, me], fetch_recv.at[chunk]).start()

        if chunk == ATTEND_AFTER:
            query_copy.wait_recv()
            attend_next()
            part_copy.start()
            stats_copy.start()

    part_copy.wait_recv()
    stats_copy.wait_recv()
    columns = jnp.concatenate(
        [stats_back[...], jnp.zeros((128 - 2 * heads, BLOCK), jnp.float32)], 0
    ).T

    for chunk in range(CHUNKS):
        wait_bytes(far.at[chunk], fetch_recv.at[chunk])

        for at in range(group):
            blocks = [own.at[chunk], far.at[chunk, 0], far.at[chunk, 1]]
            live = [None, a_live, b_live]
            h = chunk * group + at
            s = [scores(q_heads[h], pick(b, 0, at)) for b in blocks]
            s[0] = jnp.where(causal, s[0], FILL)
            top = half_max(s[0])
            for one, ok in zip(s[1:], live[1:]):
                top = jnp.maximum(top, jnp.where(ok, half_max(one), FILL))
            near_top = jnp.where(near_live, columns[:, 2 * h : 2 * h + 1], FILL)
            top = jnp.maximum(jnp.max(top, axis=1, keepdims=True) * EXP_SCALE, near_top)
            total, mixed = None, None
            for one, ok, b in zip(s, live, blocks):
                shift = top if ok is None else jnp.where(ok, top, -FILL)
                w = jnp.exp2(one * EXP_SCALE - shift)
                part = w[:, :128] + w[:, 128:]
                total = part if total is None else total + part
                part = jnp.dot(w.astype(jnp.bfloat16), pick(b, 1, at), preferred_element_type=jnp.float32)
                mixed = part if mixed is None else mixed + part
            near_total = jnp.exp2(near_top - top) * columns[:, 2 * h + 1 : 2 * h + 2]
            total = jnp.sum(total, axis=1, keepdims=True) + near_total
            mixed = mixed + part_back[h].astype(jnp.float32) * near_total
            rows = (mixed / total).astype(jnp.bfloat16)
            staged[chunk, :, :, at * HEAD_DIM : (at + 1) * HEAD_DIM] = rows.reshape(
                n_head, rows_out, HEAD_DIM
            )

        pltpu.make_async_copy(staged.at[chunk, my_head], out_slot(chunk), out_recv.at[chunk]).start()

        @pl.loop(1, n_head)
        def _(i):
            out_copy(chunk, to_head(i)).start()

    others = pl.ds(0, n_ctx - 1)
    wait_bytes(sel_all.at[others], sel_send)
    query_copy.wait_send()
    part_copy.wait_send()
    stats_copy.wait_send()
    for chunk in range(CHUNKS):
        wait_bytes(spread[chunk].at[others], spread_send.at[chunk])
        wait_bytes(send.at[chunk, others], fetch_send.at[chunk])
        wait_bytes(staged.at[chunk, pl.ds(0, n_head - 1)], out_send.at[chunk])
        wait_bytes(staged.at[chunk], out_recv.at[chunk])


def on_device(n_ctx, n_head, selected, queries, keys, values):
    heads = queries.shape[1]
    group = heads // CHUNKS
    piece = 2 * group * BLOCK // n_ctx
    bf16, dma = jnp.bfloat16, pltpu.SemaphoreType.DMA
    hbm = pl.BlockSpec(memory_space=pltpu.HBM)
    return pl.pallas_call(
        functools.partial(kernel, n_ctx, n_head, heads),
        out_shape=jax.ShapeDtypeStruct((BLOCK // n_head, n_head * heads * HEAD_DIM), bf16),
        in_specs=[pl.BlockSpec(memory_space=pltpu.SMEM), hbm, hbm, hbm],
        out_specs=pl.BlockSpec(memory_space=pl.ANY),
        scratch_shapes=[
            *[pltpu.VMEM((BLOCK, heads, HEAD_DIM), bf16)] * 3,
            dma((3,)),
            pltpu.VMEM((heads, BLOCK, HEAD_DIM), bf16),
            pltpu.VMEM((CHUNKS, n_ctx, piece, HEAD_DIM), bf16),
            pltpu.VMEM((CHUNKS, n_ctx, 2, piece, HEAD_DIM), bf16),
            pltpu.VMEM((CHUNKS, 2, n_ctx, piece, HEAD_DIM), bf16),
            pltpu.VMEM((CHUNKS, n_head, BLOCK // n_head, group * HEAD_DIM), bf16),
            pltpu.VMEM((BLOCK * heads, HEAD_DIM), jnp.float32),
            *[pltpu.VMEM((heads, BLOCK, HEAD_DIM), bf16)] * 3,
            *[pltpu.VMEM((2 * heads, BLOCK), jnp.float32)] * 2,
            pltpu.VMEM((1, 128), jnp.int32),
            pltpu.VMEM((n_ctx, 1, 128), jnp.int32),
            pltpu.SMEM((n_ctx, 1, 128), jnp.int32),
            dma, dma, dma,
            dma((CHUNKS,)), dma((CHUNKS,)),
            dma((CHUNKS,)), dma((CHUNKS,)),
            dma((3,)), dma((3,)),
            dma((CHUNKS,)), dma((CHUNKS,)),
            *[pltpu.VMEM((n_ctx, piece, HEAD_DIM), bf16)] * CHUNKS,
        ],
        compiler_params=pltpu.CompilerParams(
            collective_id=0, has_side_effects=True, vmem_limit_bytes=63 * 1024 * 1024
        ),
        name="moba",
    )(selected, queries, keys, values)


def solution(mesh):
    n_ctx, n_head = mesh.shape["ctx"], mesh.shape["head"]

    def run(queries, keys, values, selected):
        return on_device(n_ctx, n_head, selected, queries, keys, values)

    return jax.shard_map(
        run,
        mesh=mesh,
        in_specs=(
            P("ctx", "head", None),
            P("ctx", "head", None),
            P("ctx", "head", None),
            P("ctx", None),
        ),
        out_specs=P(("ctx", "head"), None),
        check_vma=False,
    )
```

```python
import functools
import math

import jax
import jax.numpy as jnp
from jax import lax
from jax.experimental import pallas as pl
from jax.experimental.pallas import tpu as pltpu
from jax.sharding import PartitionSpec as P

HEAD_DIM = 128
BLOCK = 256
CHUNKS = 4
QUERIES_AFTER = 1
ATTEND_AFTER = 1
MESH = pl.DeviceIdType.MESH
STRIDE = 27

FILL = -1e30
EXP_SCALE = HEAD_DIM ** (-0.5) * math.log2(math.e)


def kernel(
    n_ctx, n_head, heads,
    sel_ref, q_hbm, k_hbm, v_hbm, out_ref,
    q_ref, k_ref, v_ref, in_sem, q_heads, own, send, far, staged, wide,
    q_next, part, part_back, stats, stats_back,
    sel_own, sel_all, sel_smem,
    sel_send, sel_recv, sel_local, spread_send, spread_recv, fetch_send, fetch_recv,
    back_send, back_recv, out_send, out_recv,
    *spread,
):
    group = heads // CHUNKS
    pieces_of_head = n_ctx // (2 * group)
    me = lax.axis_index("ctx")
    my_head = lax.axis_index("head")
    right, left = lax.rem(me + 1, n_ctx), lax.rem(me + n_ctx - 1, n_ctx)
    rows_out = BLOCK // n_head
    cols_out = group * HEAD_DIM

    def to_ctx(i):
        return lax.rem(me + i * STRIDE, n_ctx)

    def to_head(i):
        return lax.rem(my_head + i, n_head)

    loads = [
        pltpu.make_async_copy(src, dst, in_sem.at[i])
        for i, (src, dst) in enumerate([(k_hbm, k_ref), (v_hbm, v_ref), (q_hbm, q_ref)])
    ]
    for load in loads:
        load.start()

    barrier = pltpu.get_barrier_semaphore()

    @pl.loop(1, n_ctx)
    def _(i):
        pl.semaphore_signal(barrier, inc=1, device_id={"ctx": to_ctx(i)}, device_id_type=MESH)

    @pl.loop(1, n_head)
    def _(i):
        pl.semaphore_signal(barrier, inc=1, device_id={"head": to_head(i)}, device_id_type=MESH)

    s0, s1, s2 = sel_ref[0, 0], sel_ref[0, 1], sel_ref[0, 2]
    far_a = jnp.where(s0 == me - 1, s1, s0)
    far_b = jnp.where(s2 == me - 1, s1, s2)
    lane = lax.broadcasted_iota(jnp.int32, (1, 128), 1)
    sel_own[...] = jnp.where(lane == 0, far_a, far_b)

    def split_heads(src, store, first, count):
        wide[...] = src[...].astype(jnp.float32).reshape(BLOCK * heads, HEAD_DIM)
        for h in range(first, first + count):
            store(h, wide[pl.ds(h, BLOCK, stride=heads), :].astype(jnp.bfloat16))

    def store_own(kind):
        def store(h, rows):
            chunk, at = divmod(h, group)
            start = (kind * group + at) * pieces_of_head
            own[chunk, pl.ds(start, pieces_of_head)] = rows.reshape(
                pieces_of_head, BLOCK // pieces_of_head, HEAD_DIM
            )
        return store

    def store_q(h, rows):
        q_heads[h] = rows

    def spread_copy(chunk, peer):
        return pltpu.make_async_remote_copy(
            src_ref=own.at[chunk, peer], dst_ref=spread[chunk].at[me],
            send_sem=spread_send.at[chunk], recv_sem=spread_recv.at[chunk],
            device_id={"ctx": peer}, device_id_type=MESH,
        )

    def pass_copy(at, src, dst, peer):
        return pltpu.make_async_remote_copy(
            src_ref=src, dst_ref=dst, send_sem=back_send.at[at], recv_sem=back_recv.at[at],
            device_id={"ctx": peer}, device_id_type=MESH,
        )

    query_copy = pass_copy(0, q_heads, q_next, left)
    part_copy = pass_copy(1, part, part_back, right)
    stats_copy = pass_copy(2, stats, stats_back, right)

    def sel_copy(peer):
        return pltpu.make_async_remote_copy(
            src_ref=sel_own, dst_ref=sel_all.at[me],
            send_sem=sel_send, recv_sem=sel_recv,
            device_id={"ctx": peer}, device_id_type=MESH,
        )

    def fetch_copy(chunk, peer):
        return pltpu.make_async_remote_copy(
            src_ref=send.at[chunk, peer], dst_ref=far.at[chunk, me],
            send_sem=fetch_send.at[chunk], recv_sem=fetch_recv.at[chunk],
            device_id={"ctx": peer}, device_id_type=MESH,
        )

    def out_slot(chunk):
        return out_ref.at[:, pl.ds(pl.multiple_of(my_head * (heads * HEAD_DIM) + chunk * cols_out, HEAD_DIM), cols_out)]

    def out_copy(chunk, peer):
        return pltpu.make_async_remote_copy(
            src_ref=staged.at[chunk, peer], dst_ref=out_slot(chunk),
            send_sem=out_send.at[chunk], recv_sem=out_recv.at[chunk],
            device_id={"head": peer}, device_id_type=MESH,
        )

    def wait_bytes(ref, sem):
        pltpu.make_async_copy(ref, ref, sem).wait()

    loads[0].wait()
    split_heads(k_ref, store_own(0), 0, heads)
    loads[1].wait()
    split_heads(v_ref, store_own(1), 0, heads)

    loads[2].wait()
    split_heads(q_ref, store_q, 0, heads)

    pl.semaphore_wait(barrier, n_ctx - 1 + n_head - 1)

    pltpu.make_async_copy(sel_own, sel_all.at[me], sel_recv).start()

    @pl.loop(1, n_ctx)
    def _(i):
        sel_copy(to_ctx(i)).start()

    for chunk in range(CHUNKS):
        pltpu.make_async_copy(own.at[chunk, me], spread[chunk].at[me], spread_recv.at[chunk]).start()

        @pl.loop(1, n_ctx)
        def _(i):
            spread_copy(chunk, to_ctx(i)).start()

        if chunk == QUERIES_AFTER:
            query_copy.start()


    wait_bytes(sel_all, sel_recv)
    sel_down = pltpu.make_async_copy(sel_all, sel_smem, sel_local)
    sel_down.start()
    sel_down.wait()

    causal = lax.broadcasted_iota(jnp.int32, (BLOCK, BLOCK), 1) <= lax.broadcasted_iota(
        jnp.int32, (BLOCK, BLOCK), 0
    )
    near_live, a_live, b_live = me >= 1, far_a != me, far_b != me
    stat_lane = lax.broadcasted_iota(jnp.int32, (BLOCK, 128), 1)

    def scores(q, k):
        return lax.dot_general(q, k, (((1,), (1,)), ((), ())), preferred_element_type=jnp.float32)

    def half_max(s):
        return jnp.maximum(s[:, :128], s[:, 128:])

    def pick(buf, kind, at):
        first = (kind * group + at) * pieces_of_head
        return buf[pl.ds(first, pieces_of_head)].reshape(BLOCK, HEAD_DIM)

    def attend_next():
        columns = jnp.zeros((BLOCK, 128), jnp.float32)
        for h in range(heads):
            chunk, at = divmod(h, group)
            s = scores(q_next[h], pick(own.at[chunk], 0, at))
            top = jnp.max(half_max(s), axis=1, keepdims=True) * EXP_SCALE
            w = jnp.exp2(s * EXP_SCALE - top)
            total = jnp.sum(w[:, :128] + w[:, 128:], axis=1, keepdims=True)
            mixed = jnp.dot(
                w.astype(jnp.bfloat16), pick(own.at[chunk], 1, at), preferred_element_type=jnp.float32
            )
            part[h] = (mixed / total).astype(jnp.bfloat16)
            columns = jnp.where(stat_lane == 2 * h, top, columns)
            columns = jnp.where(stat_lane == 2 * h + 1, total, columns)
        stats[...] = columns.T[: 2 * heads]

    for chunk in range(CHUNKS):
        wait_bytes(spread[chunk], spread_recv.at[chunk])

        def fill(peer):
            for slot in range(2):
                send[chunk, peer, slot] = spread[chunk][sel_smem[peer, 0, slot]]

        @pl.loop(1, n_ctx)
        def _(i):
            peer = to_ctx(i)
            fill(peer)
            fetch_copy(chunk, peer).start()

        fill(me)
        pltpu.make_async_copy(send.at[chunk, me], far.at[chunk, me], fetch_recv.at[chunk]).start()

        if chunk == ATTEND_AFTER:
            query_copy.wait_recv()
            attend_next()
            part_copy.start()
            stats_copy.start()

    part_copy.wait_recv()
    stats_copy.wait_recv()
    columns = jnp.concatenate(
        [stats_back[...], jnp.zeros((128 - 2 * heads, BLOCK), jnp.float32)], 0
    ).T

    for chunk in range(CHUNKS):
        wait_bytes(far.at[chunk], fetch_recv.at[chunk])

        for at in range(group):
            blocks = [own.at[chunk], far.at[chunk, :, 0], far.at[chunk, :, 1]]
            live = [None, a_live, b_live]
            h = chunk * group + at
            s = [scores(q_heads[h], pick(b, 0, at)) for b in blocks]
            s[0] = jnp.where(causal, s[0], FILL)
            top = half_max(s[0])
            for one, ok in zip(s[1:], live[1:]):
                top = jnp.maximum(top, jnp.where(ok, half_max(one), FILL))
            near_top = jnp.where(near_live, columns[:, 2 * h : 2 * h + 1], FILL)
            top = jnp.maximum(jnp.max(top, axis=1, keepdims=True) * EXP_SCALE, near_top)
            total, mixed = None, None
            for one, ok, b in zip(s, live, blocks):
                shift = top if ok is None else jnp.where(ok, top, -FILL)
                w = jnp.exp2(one * EXP_SCALE - shift)
                part = w[:, :128] + w[:, 128:]
                total = part if total is None else total + part
                part = jnp.dot(w.astype(jnp.bfloat16), pick(b, 1, at), preferred_element_type=jnp.float32)
                mixed = part if mixed is None else mixed + part
            near_total = jnp.exp2(near_top - top) * columns[:, 2 * h + 1 : 2 * h + 2]
            total = jnp.sum(total, axis=1, keepdims=True) + near_total
            mixed = mixed + part_back[h].astype(jnp.float32) * near_total
            rows = (mixed / total).astype(jnp.bfloat16)
            staged[chunk, :, :, at * HEAD_DIM : (at + 1) * HEAD_DIM] = rows.reshape(
                n_head, rows_out, HEAD_DIM
            )

        pltpu.make_async_copy(staged.at[chunk, my_head], out_slot(chunk), out_recv.at[chunk]).start()

        @pl.loop(1, n_head)
        def _(i):
            out_copy(chunk, to_head(i)).start()

    others = pl.ds(0, n_ctx - 1)
    wait_bytes(sel_all.at[others], sel_send)
    query_copy.wait_send()
    part_copy.wait_send()
    stats_copy.wait_send()
    for chunk in range(CHUNKS):
        wait_bytes(spread[chunk].at[others], spread_send.at[chunk])
        wait_bytes(send.at[chunk, others], fetch_send.at[chunk])
        wait_bytes(staged.at[chunk, pl.ds(0, n_head - 1)], out_send.at[chunk])
        wait_bytes(staged.at[chunk], out_recv.at[chunk])


def on_device(n_ctx, n_head, selected, queries, keys, values):
    heads = queries.shape[1]
    group = heads // CHUNKS
    piece = 2 * group * BLOCK // n_ctx
    bf16, dma = jnp.bfloat16, pltpu.SemaphoreType.DMA
    hbm = pl.BlockSpec(memory_space=pltpu.HBM)
    return pl.pallas_call(
        functools.partial(kernel, n_ctx, n_head, heads),
        out_shape=jax.ShapeDtypeStruct((BLOCK // n_head, n_head * heads * HEAD_DIM), bf16),
        in_specs=[pl.BlockSpec(memory_space=pltpu.SMEM), hbm, hbm, hbm],
        out_specs=pl.BlockSpec(memory_space=pl.ANY),
        scratch_shapes=[
            *[pltpu.VMEM((BLOCK, heads, HEAD_DIM), bf16)] * 3,
            dma((3,)),
            pltpu.VMEM((heads, BLOCK, HEAD_DIM), bf16),
            pltpu.VMEM((CHUNKS, n_ctx, piece, HEAD_DIM), bf16),
            pltpu.VMEM((CHUNKS, n_ctx, 2, piece, HEAD_DIM), bf16),
            pltpu.VMEM((CHUNKS, n_ctx, 2, piece, HEAD_DIM), bf16),
            pltpu.VMEM((CHUNKS, n_head, BLOCK // n_head, group * HEAD_DIM), bf16),
            pltpu.VMEM((BLOCK * heads, HEAD_DIM), jnp.float32),
            *[pltpu.VMEM((heads, BLOCK, HEAD_DIM), bf16)] * 3,
            *[pltpu.VMEM((2 * heads, BLOCK), jnp.float32)] * 2,
            pltpu.VMEM((1, 128), jnp.int32),
            pltpu.VMEM((n_ctx, 1, 128), jnp.int32),
            pltpu.SMEM((n_ctx, 1, 128), jnp.int32),
            dma, dma, dma,
            dma((CHUNKS,)), dma((CHUNKS,)),
            dma((CHUNKS,)), dma((CHUNKS,)),
            dma((3,)), dma((3,)),
            dma((CHUNKS,)), dma((CHUNKS,)),
            *[pltpu.VMEM((n_ctx, piece, HEAD_DIM), bf16)] * CHUNKS,
        ],
        compiler_params=pltpu.CompilerParams(
            collective_id=0, has_side_effects=True, vmem_limit_bytes=63 * 1024 * 1024
        ),
        name="moba",
    )(selected, queries, keys, values)


def solution(mesh):
    n_ctx, n_head = mesh.shape["ctx"], mesh.shape["head"]

    def run(queries, keys, values, selected):
        return on_device(n_ctx, n_head, selected, queries, keys, values)

    return jax.shard_map(
        run,
        mesh=mesh,
        in_specs=(
            P("ctx", "head", None),
            P("ctx", "head", None),
            P("ctx", "head", None),
            P("ctx", None),
        ),
        out_specs=P(("ctx", "head"), None),
        check_vma=False,
    )
```
